32 devices in a mesh: grp: 2 (over x), ep: 16 (over z, y, core).
Axes of the slice: x: 2, y: 2, z: 4, core: 2. Of those that a mesh axis runs over, the one named last changes fastest.
Arguments:
- upstream: bfloat16 [4096, 2048], P(('grp', 'ep')), parts along dimension 0, may hold values from -6 to 6
- inputs: bfloat16 [4096, 2048], P(('grp', 'ep')), parts along dimension 0, may hold values from -6 to 6
- expert_ids: int32 [4096, 2], P(('grp', 'ep')), parts along dimension 0, may hold values from 0 to 7, all different within a row; in each aligned block of 128 rows (0 to 127, 128 to 255, ...) at most 48 rows name the same one
- gate_weights: bfloat16 [4096, 2], P(('grp', 'ep')), parts along dimension 0, may hold values from 0.099609375 to 1
- w_in: bfloat16 [16, 2048, 768], P('ep'), may hold values from -0.125 to 0.125
- w_down: bfloat16 [16, 384, 2048], P('ep'), may hold values from -0.21875 to 0.21875
Outputs:
- grad_inputs: bfloat16 [4096, 2048], P(('grp', 'ep')), parts along dimension 0
- grad_gates: float32 [4096, 2], P(('grp', 'ep')), parts along dimension 0
- grad_w_in: bfloat16 [32, 2048, 768], P(('grp', 'ep')), parts along dimension 0
- grad_w_down: bfloat16 [32, 384, 2048], P(('grp', 'ep')), parts along dimension 0
The draws below stay inside these ranges and needn't reach their ends.
There are 2 independent parts, one for each index of `grp`. The reference program is written for one: setup_inputs(seed, part) draws one part's arguments, and reference() takes and returns one part's arrays. A program takes and returns all parts, laid end to end along the dimension named above; an argument that names none is the same for every part. Nothing has to cross between parts.
Inputs may be any that keep to these rules, and one draw needn't show every extreme that they name: `expert_ids`: each token names 2 different experts, every expert is named by some token, and among the tokens of one index of ep no expert is named more than 48 times; some expert is named exactly 48 times in some such block.
All inputs are finite; a program needn't handle non-finite values.
Results may differ from the reference program's by a relative error of at most 0.0067.
Values may be sent and summed in bfloat16 or wider, within the bound.
No kernel may reach another device: no remote copies, remote signals or barrier semaphores. Data moves between devices by JAX's collectives and lax.ppermute only.
A program may use at most 128 MiB of HBM per device.

```python
import math
import jax
import jax.numpy as jnp
import numpy as np
from jax import lax

D = 2048
FF = 768
TOP = 2
TOK_DEV = 128
EXPERTS = 8
TOKENS = 2048
CAP = 48
ROUTED = 512
N_EP = 16


def block_scale(rng, extent, split, least, high):
    def one(axis_at, shards_of):
        draws = jax.random.uniform(jax.random.fold_in(jax.random.fold_in(rng, 6), axis_at), (shards_of,), jnp.float32, least / len(split), high / len(split))
        return jnp.repeat(jnp.exp(draws), extent[axis_at] // shards_of).reshape((-1,) + (1,) * (len(extent) - axis_at - 1))

    factor_of = one(*split[0])
    for cut in split[1:]:
        factor_of = factor_of * one(*cut)
    return factor_of


def shared_out(stream_key, own, number, rows, number_of, top, limit, slope):
    order = jax.random.permutation(stream_key, number_of)
    heavy_load, ordinary = load_shares(number_of, rows * top, limit, slope, True), load_shares(number_of, rows * top, limit, slope, False)
    places = jnp.arange(number_of)

    def named(tallies, offset_by):
        used = int((tallies > 0).sum())
        fixed = max(1, used // 4)
        moved = fixed + (places - fixed + offset_by * (used - fixed)) % max(1, number_of - fixed)
        return jnp.zeros((number_of,), jnp.int32).at[order[jnp.where(places < fixed, places, moved)]].set(jnp.asarray(tallies, jnp.int32))

    tallies = jnp.where(number % 4 == 0, named(heavy_load, number // 4), named(ordinary, number - number // 4 - 1))
    mixed = jax.random.permutation(jax.random.fold_in(own, 3), number_of)
    source_of, sink = mixed[0:number_of // 2 * 2:2], mixed[1:number_of // 2 * 2:2]
    margin = jnp.minimum(tallies[source_of] - 1, limit - tallies[sink]) // 2
    margin = jnp.where((source_of == order[0]) | (sink == order[0]) | (tallies[sink] == 0), 0, jnp.maximum(margin, 0))
    moved = jax.random.randint(jax.random.fold_in(own, 4), (number_of // 2,), 0, 1 << 20) % (margin + 1)
    tallies = tallies.at[source_of].add(-moved).at[sink].add(moved)
    items = jnp.searchsorted(jnp.cumsum(tallies), jnp.arange(rows * top), side="right").astype(jnp.int32)
    table = items.reshape(top, rows).T
    table = table[jax.random.permutation(jax.random.fold_in(own, 1), rows)]
    offset_by = jax.random.randint(jax.random.fold_in(own, 2), (rows, 1), 0, top)
    return jnp.take_along_axis(table, (jnp.arange(top)[None, :] + offset_by) % top, axis=1)


def load_shares(number_of, total, reach, lean, full):
    weights = [(1 << 20) // math.isqrt(standing ** lean) + 1 for standing in range(1, number_of + 1)]
    largest = reach if full else min(reach, max(-(-total // number_of), total * weights[0] // sum(weights)))
    least = 1 if total - largest >= number_of - 1 else 0
    holding, spare = [largest] + [least] * (number_of - 1), total - largest - least * (number_of - 1)
    while spare > 0:
        movable = [i for i in range(1, number_of) if holding[i] < largest] or [i for i in range(1, number_of) if holding[i] < reach]
        whole, left = sum([weights[i] for i in movable]), spare
        for i in movable:
            extra = min(reach - holding[i], max(1, left * weights[i] // whole), spare)
            holding[i] = holding[i] + extra
            spare = spare - extra
    return np.array(holding)


def scatter_about(key, dims, scale, bound, shards=(), held_as=jnp.bfloat16):
    entries = jax.random.normal(key, dims, jnp.float32) * scale
    if len(shards) > 0:
        entries = block_scale(key, dims, shards, -0.22, 0.18) * entries
    return jnp.clip(entries, min=-bound, max=bound).astype(held_as)


def setup_inputs(seed: int = 0, part: int = 0) -> dict:
    seeds = jax.random.split(jax.random.key(seed), 7)
    part_keys = jax.random.split(jax.random.fold_in(seeds[6], part), 7)
    upstream = scatter_about(part_keys[0], (TOKENS, D), 1.0, 6.0, ((0, 16),))
    inputs = scatter_about(part_keys[1], (TOKENS, D), 1.0, 6.0, ((0, 16),))
    expert_ids_keys = jax.random.split(jax.random.fold_in(part_keys[2], 1), TOKENS // TOK_DEV)
    expert_ids_turns = jax.random.permutation(jax.random.fold_in(part_keys[2], 3), TOKENS // TOK_DEV)
    expert_ids = jax.vmap(lambda own, number: shared_out(jax.random.fold_in(part_keys[2], 2), own, number, TOK_DEV, EXPERTS, TOP, CAP, 2))(expert_ids_keys, expert_ids_turns).reshape((TOKENS, TOP))
    gate_weights = jnp.clip(0.099609375 + 0.9003906 * jax.random.uniform(part_keys[3], (TOKENS, TOP), jnp.float32) ** block_scale(part_keys[3], (TOKENS, TOP), ((0, 16),), -0.2, 0.2), 0.099609375, 1.0).astype(jnp.bfloat16)
    w_in = scatter_about(seeds[4], (EXPERTS * 2, D, FF), D ** -0.5, 0.125, ((0, 16),))
    w_down = scatter_about(seeds[5], (EXPERTS * 2, FF // 2, D), FF ** -0.5, 0.21875, ((0, 16),))
    return dict(upstream=upstream, inputs=inputs, expert_ids=expert_ids, gate_weights=gate_weights, w_in=w_in, w_down=w_down)


def half_terms(token_rows, grad_rows, gate_rows, weight_in, weight_down, factor):
    halfwidth = weight_down.shape[0]
    gate_up = jnp.dot(token_rows, weight_in, preferred_element_type=jnp.float32)
    gate_pre = gate_up[:, :halfwidth]
    up_pre = gate_up[:, halfwidth:]
    squash = jax.nn.sigmoid(gate_pre)
    active = gate_pre * squash
    hidden = active * up_pre
    pulled = lax.dot_general(grad_rows, weight_down, (((1,), (1,)), ((), ())), preferred_element_type=jnp.float32)
    gate_col = gate_rows.astype(jnp.float32)[:, None]
    gate_part = lax.optimization_barrier(jnp.sum(hidden * pulled, axis=1)).astype(jnp.bfloat16)
    hidden_grad = gate_col * pulled
    gate_grad = hidden_grad * up_pre * squash * (1.0 + gate_pre * (1.0 - squash))
    up_grad = hidden_grad * active
    pre_grad = jnp.concatenate([gate_grad, up_grad], axis=1).astype(jnp.bfloat16)
    scaled = (gate_col * hidden).astype(jnp.bfloat16)
    grad_in = lax.dot_general(token_rows, pre_grad, (((0,), (0,)), ((), ())), preferred_element_type=jnp.float32)
    grad_down = lax.dot_general(scaled, grad_rows, (((0,), (0,)), ((), ())), preferred_element_type=jnp.float32)
    returned = lax.dot_general(pre_grad, weight_in, (((1,), (1,)), ((), ())), preferred_element_type=jnp.float32)
    return ((grad_in * factor).astype(jnp.bfloat16), (grad_down * factor).astype(jnp.bfloat16), returned.astype(jnp.bfloat16), gate_part)

def reference(upstream, inputs, expert_ids, gate_weights, w_in, w_down):
    routed = TOKENS * TOP
    room = N_EP * CAP
    flat_ids = expert_ids.reshape(routed).astype(jnp.int32)
    onehot = (flat_ids[:, None] == jnp.arange(EXPERTS, dtype=jnp.int32)[None, :]).astype(jnp.int32)
    earlier = jnp.cumsum(onehot, axis=0) - onehot
    position = lax.optimization_barrier(jnp.sum(earlier * onehot, axis=1)).astype(jnp.int32)
    target = (flat_ids * room + position).astype(jnp.int32)
    source = jnp.full((EXPERTS * room,), routed, jnp.int32).at[target].set(jnp.arange(routed, dtype=jnp.int32))
    filled = source < routed
    token_of = jnp.where(filled, source // TOP, TOKENS).astype(jnp.int32)
    zero_row = jnp.zeros((1, D), upstream.dtype)
    x_buffer = jnp.concatenate([inputs, zero_row], axis=0)[token_of].reshape(EXPERTS, room, D)
    up_buffer = jnp.concatenate([upstream, zero_row], axis=0)[token_of].reshape(EXPERTS, room, D)
    gate_flat = jnp.concatenate([gate_weights.reshape(routed), jnp.zeros((1,), gate_weights.dtype)], axis=0)
    gate_buffer = gate_flat[source].reshape(EXPERTS, room)
    factor = 1.0 / math.sqrt(ROUTED)

    def per_expert(pieces):
        token_rows, grad_rows, gate_rows, pair_in, pair_down = pieces
        first = half_terms(token_rows, grad_rows, gate_rows, pair_in[0], pair_down[0], factor)
        second = half_terms(token_rows, grad_rows, gate_rows, pair_in[1], pair_down[1], factor)
        return tuple((jnp.stack([first[n], second[n]], axis=0) for n in range(4)))
    grad_in, grad_down, returned, gate_part = lax.map(per_expert, (x_buffer, up_buffer, gate_buffer, w_in.reshape(EXPERTS, 2, D, FF), w_down.reshape(EXPERTS, 2, FF // 2, D)))
    summed = (returned[:, 0].astype(jnp.float32) + returned[:, 1].astype(jnp.float32)).astype(jnp.bfloat16).reshape(EXPERTS * room, D)
    gate_sum = (gate_part[:, 0].astype(jnp.float32) + gate_part[:, 1].astype(jnp.float32)).reshape(EXPERTS * room)
    grad_inputs = lax.optimization_barrier(jnp.sum(summed[target].astype(jnp.float32).reshape(TOKENS, TOP, D), axis=1)).astype(jnp.bfloat16)
    grad_gates = gate_sum[target].reshape(TOKENS, TOP)
    return (grad_inputs, grad_gates, grad_in.reshape(EXPERTS * 2, D, FF), grad_down.reshape(EXPERTS * 2, FF // 2, D))
```

```python
import functools
import math

import jax
import jax.numpy as jnp
from jax import lax
from jax.experimental import pallas as pl
from jax.experimental.pallas import tpu as pltpu
from jax.sharding import PartitionSpec as P

F32 = jnp.float32
BF16 = jnp.bfloat16
LANES = 128
VMEM_LIMIT = 40 * 1024 * 1024


def dot(a, b, contract):
    return lax.dot_general(a, b, ((contract[:1], contract[1:]), ((), ())), preferred_element_type=F32)


def places(ids, experts):
    choose, tokens = ids.shape
    names = lax.broadcasted_iota(jnp.int32, (experts, tokens), 0)
    marks = [(names == ids[k : k + 1, :]).astype(F32) for k in range(choose)]
    earlier = lax.broadcasted_iota(jnp.int32, (tokens, tokens), 0) < lax.broadcasted_iota(
        jnp.int32, (tokens, tokens), 1
    )
    counts = dot(sum(marks).astype(BF16), earlier.astype(BF16), (1, 0))
    return [jnp.sum(counts * mark, axis=0, keepdims=True).astype(jnp.int32) for mark in marks]


def picks(ids, place, expert, first, rows):
    choose, tokens = ids.shape
    slot = lax.broadcasted_iota(jnp.int32, (rows, tokens), 0) + first
    return [
        ((ids[k : k + 1, :] == expert) & (place[k] == slot)).astype(F32) for k in range(choose)
    ]


def pack_kernel(experts, first, rows, chip_ref, ids_ref, gates_ref, x_ref, up_ref, *out_refs):
    width = x_ref.shape[1]
    ids = ids_ref[...]
    gates = gates_ref[...].astype(F32)
    place = places(ids, experts)
    chip = chip_ref[0]
    plain, gated = [], []
    for step in range(experts):
        ones = picks(ids, place, chip ^ step, first, rows)
        plain.append(sum(ones))
        gated.append(sum(one * gates[k : k + 1, :] for k, one in enumerate(ones)))
    x_rows = dot(jnp.concatenate(plain, axis=0).astype(BF16), x_ref[...], (1, 0)).astype(BF16)
    up_rows = dot(jnp.concatenate(gated, axis=0).astype(BF16), up_ref[...], (1, 0)).astype(BF16)
    for step in range(experts):
        out_refs[step][:, :width] = x_rows[step * rows : (step + 1) * rows]
        out_refs[step][:, width:] = up_rows[step * rows : (step + 1) * rows]


def expert_kernel(blocks, rows, *refs):
    ins, outs = refs[:blocks], refs[blocks + 4 :]
    w_in_refs, w_down_refs = refs[blocks : blocks + 2], refs[blocks + 2 : blocks + 4]
    back_refs = outs[:blocks]
    x_out, up_out, grad_refs, hidden_refs = outs[blocks], outs[blocks + 1], outs[blocks + 2 : blocks + 4], outs[blocks + 4 : blocks + 6]
    width = x_out.shape[1]
    half = w_down_refs[0].shape[0]
    for b in range(blocks):
        x_out[b * rows : (b + 1) * rows, :] = ins[b][:, :width]
        up_out[b * rows : (b + 1) * rows, :] = ins[b][:, width:]
    x_rows, up_rows = x_out[...], up_out[...]
    gate_parts = []
    for w_in_ref, w_down_ref, grad_ref, hidden_ref in zip(w_in_refs, w_down_refs, grad_refs, hidden_refs):
        pre = dot(x_rows, w_in_ref[...], (1, 0))
        pulled = dot(up_rows, w_down_ref[...], (1, 1))
        gate_pre, up_pre = pre[:, :half], pre[:, half:]
        squash = jax.nn.sigmoid(gate_pre)
        active = gate_pre * squash
        hidden = active * up_pre
        gate_parts.append(jnp.sum(hidden * pulled, axis=1, keepdims=True))
        grad_ref[:, :half] = (pulled * up_pre * squash * (1.0 + gate_pre * (1.0 - squash))).astype(BF16)
        grad_ref[:, half:] = (pulled * active).astype(BF16)
        hidden_ref[...] = hidden.astype(BF16)
    back = sum(
        dot(grad_ref[...], w_in_ref[...], (1, 1)) for grad_ref, w_in_ref in zip(grad_refs, w_in_refs)
    ).astype(BF16)
    lane = lax.broadcasted_iota(jnp.int32, (blocks * rows, LANES), 1)
    gate_lanes = jnp.where(lane == 0, gate_parts[0], jnp.where(lane == 1, gate_parts[1], 0.0)).astype(BF16)
    for b in range(blocks):
        back_refs[b][:, :width] = back[b * rows : (b + 1) * rows]
        back_refs[b][:, width:] = gate_lanes[b * rows : (b + 1) * rows]


def weight_kernel(chunks, scale, *refs):
    lefts, rights, rest = refs[:chunks], refs[chunks : 2 * chunks], refs[2 * chunks :]
    total = sum(dot(left[...], right[...], (0, 0)) for left, right in zip(lefts, rights))
    if scale is not None:
        total = (total + rest[0][...].astype(F32)) * scale
    rest[-1][...] = total.astype(BF16)


def combine_kernel(experts, spans, chip_ref, ids_ref, gates_ref, *refs):
    blocks, (out_ref, gate_ref) = refs[:-2], refs[-2:]
    width = out_ref.shape[1]
    ids = ids_ref[...]
    choose = ids.shape[0]
    place = places(ids, experts)
    chip = chip_ref[0]
    ones = [[] for _ in range(choose)]
    values = []
    at = 0
    for first, rows in spans:
        for step in range(experts):
            for k, one in enumerate(picks(ids, place, chip ^ step, first, rows)):
                ones[k].append(one)
            values.append(blocks[at][...])
            at += 1
    ones = [jnp.concatenate(one, axis=0).astype(BF16) for one in ones]
    rows_in = jnp.concatenate(values, axis=0)
    out_ref[...] = dot(sum(ones), rows_in[:, :width], (0, 0)).astype(BF16)
    for k in range(choose):
        parts = dot(rows_in[:, width:], ones[k], (0, 0))
        gate_ref[k : k + 1, :] = (parts[0:1, :] + parts[1:2, :]) / gates_ref[k : k + 1, :].astype(F32)


def whole():
    return pl.BlockSpec(memory_space=pltpu.VMEM)


def call(kernel, out_shape, scalars, *args, flops=0):
    nbytes = sum(a.size * a.dtype.itemsize for a in args) + sum(
        math.prod(o.shape) * o.dtype.itemsize for o in out_shape
    )
    return pl.pallas_call(
        kernel,
        out_shape=tuple(out_shape),
        in_specs=[pl.BlockSpec(memory_space=pltpu.SMEM)] * len(scalars) + [whole()] * len(args),
        out_specs=tuple(whole() for _ in out_shape),
        compiler_params=pltpu.CompilerParams(vmem_limit_bytes=VMEM_LIMIT),
        cost_estimate=pl.CostEstimate(flops=flops, bytes_accessed=nbytes, transcendentals=0),
    )(*scalars, *args)


def weight_grad(lefts, rights, received=None, scale=None):
    rows_of = [left.shape[0] for left in lefts]
    depth, columns = lefts[0].shape[1], rights[0].shape[1]
    tile = 512 if depth % 512 == 0 else depth
    if depth <= 512:
        tile = 128
    in_specs = [pl.BlockSpec((r, tile), lambda i: (0, i)) for r in rows_of]
    in_specs += [pl.BlockSpec((r, columns), lambda i: (0, 0)) for r in rows_of]
    args = [*lefts, *rights]
    if received is not None:
        in_specs.append(pl.BlockSpec((tile, columns), lambda i: (i, 0)))
        args.append(received)
    return pl.pallas_call(
        functools.partial(weight_kernel, len(lefts), scale),
        grid=(depth // tile,),
        out_shape=jax.ShapeDtypeStruct((depth, columns), BF16),
        in_specs=in_specs,
        out_specs=pl.BlockSpec((tile, columns), lambda i: (i, 0)),
        compiler_params=pltpu.CompilerParams(vmem_limit_bytes=VMEM_LIMIT),
        cost_estimate=pl.CostEstimate(
            flops=2 * sum(rows_of) * depth * columns,
            bytes_accessed=2 * (sum(rows_of) * (depth + columns) + depth * columns),
            transcendentals=0,
        ),
    )(*args)


def per_device(upstream, inputs, expert_ids, gate_weights, w_in, w_down):
    devices = lax.axis_size("ep")
    experts = devices // 2
    tokens, features = upstream.shape
    choose = expert_ids.shape[1]
    routed = tokens * choose
    capacity = routed * 3 // devices
    half = w_down.shape[1]
    room = -(-capacity // 16) * 16
    spans = [(0, room)] if room <= 16 else [(0, room - 16), (room - 16, 16)]
    chip = (lax.axis_index("ep") // 2).astype(jnp.int32).reshape(1)
    ids, gates = expert_ids.T, gate_weights.T
    factor = 1.0 / math.sqrt(2 * routed)

    def swap(value):
        return lax.ppermute(value, "ep", [(d, d ^ 1) for d in range(devices)])

    def exchange(blocks):
        return [
            block if step == 0 else lax.ppermute(block, "ep", [(d, d ^ (2 * step)) for d in range(devices)])
            for step, block in enumerate(blocks)
        ]

    own_in, own_down = w_in[0], w_down[0]
    other_in, other_down = swap(own_in), swap(own_down)

    arrived = []
    for first, rows in spans:
        sent = call(
            functools.partial(pack_kernel, experts, first, rows),
            [jax.ShapeDtypeStruct((rows, 2 * features), BF16)] * experts,
            [chip],
            ids,
            gates,
            inputs,
            upstream,
            flops=4 * rows * experts * tokens * features,
        )
        arrived.append(exchange(sent))

    returned, x_all, up_all, own_grad, other_grad, own_hidden, other_hidden = [], [], [], [], [], [], []
    for (first, rows), blocks in zip(spans, arrived):
        total = rows * experts
        out = call(
            functools.partial(expert_kernel, experts, rows),
            [jax.ShapeDtypeStruct((rows, features + LANES), BF16)] * experts
            + [jax.ShapeDtypeStruct((total, features), BF16)] * 2
            + [jax.ShapeDtypeStruct((total, 2 * half), BF16)] * 2
            + [jax.ShapeDtypeStruct((total, half), BF16)] * 2,
            [],
            *blocks,
            own_in,
            other_in,
            own_down,
            other_down,
            flops=20 * total * half * features,
        )
        returned += exchange(out[:experts])
        for keep, value in zip((x_all, up_all, own_grad, other_grad, own_hidden, other_hidden), out[experts:]):
            keep.append(value)

    other_part_in = swap(weight_grad(x_all, other_grad))
    other_part_down = swap(weight_grad(other_hidden, up_all))
    grad_in = weight_grad(x_all, own_grad, other_part_in, factor)
    grad_down = weight_grad(own_hidden, up_all, other_part_down, factor)

    grad_inputs, grad_gates = call(
        functools.partial(combine_kernel, experts, spans),
        [jax.ShapeDtypeStruct((tokens, features), BF16), jax.ShapeDtypeStruct((choose, tokens), F32)],
        [chip],
        ids,
        gates,
        *returned,
        flops=2 * room * experts * tokens * features,
    )
    return (grad_inputs, grad_gates.T, grad_in[None], grad_down[None])


def solution(mesh):
    rows = P(("grp", "ep"), None)
    return jax.shard_map(
        per_device,
        mesh=mesh,
        in_specs=(rows, rows, rows, rows, P("ep", None, None), P("ep", None, None)),
        out_specs=(rows, rows, P(("grp", "ep"), None, None), P(("grp", "ep"), None, None)),
        check_vma=False,
    )
```

```python
import functools
import math

import jax
import jax.numpy as jnp
from jax import lax
from jax.experimental import pallas as pl
from jax.experimental.pallas import tpu as pltpu
from jax.sharding import PartitionSpec as P

F32 = jnp.float32
BF16 = jnp.bfloat16
LANES = 128
MIB = 1024 * 1024
ORDER = (1, 2, 6, 4, 7, 5, 3)
SLAB = 512
EARLY = 3


def dot(a, b, contract):
    return lax.dot_general(a, b, ((contract[:1], contract[1:]), ((), ())), preferred_element_type=F32)


def places(ids, experts):
    choose, tokens = ids.shape
    names = lax.broadcasted_iota(jnp.int32, (experts, tokens), 0)
    marks = [(names == ids[k : k + 1, :]).astype(F32) for k in range(choose)]
    earlier = lax.broadcasted_iota(jnp.int32, (tokens, tokens), 0) < lax.broadcasted_iota(
        jnp.int32, (tokens, tokens), 1
    )
    counts = dot(sum(marks).astype(BF16), earlier.astype(BF16), (1, 0))
    return [jnp.sum(counts * mark, axis=0, keepdims=True).astype(jnp.int32) for mark in marks]


def picks(ids, place, expert, first, rows):
    choose, tokens = ids.shape
    slot = lax.broadcasted_iota(jnp.int32, (rows, tokens), 0) + first
    return [
        ((ids[k : k + 1, :] == expert) & (place[k] == slot)).astype(F32) for k in range(choose)
    ]


def load(pairs, sems):
    copies = [pltpu.make_async_copy(a, b, sems.at[n]) for n, (a, b) in enumerate(pairs)]
    for copy in copies:
        copy.start()
    return copies


def targets(steps, experts, chip):
    return [chip ^ n if steps else n for n in range(experts)]


def rows_of(chip, step, rows):
    return pl.ds(pl.multiple_of((chip ^ step) * rows, 16), rows)


def pack_kernel(experts, rows, steps, with_x, held, chip_ref, *refs):
    hbm, refs = refs[: 3 + with_x], refs[3 + with_x + held :]
    sends, kept_ones = len(steps) + with_x, 2 * with_x
    ones_refs, refs = refs[sends : sends + kept_ones], refs[:sends] + refs[sends + kept_ones :]
    outs, local, sends_local, sems = refs[:sends], refs[sends : 2 * sends + 3 + with_x][: 3 + with_x], refs[-1 - sends : -1], refs[-1]
    copies = load(zip(hbm, local), sems)
    copies[0].wait()
    copies[1].wait()
    ids = local[0][...]
    gates = local[1][...].astype(F32)
    place = places(ids, experts)
    chip = chip_ref[0]
    gated = [
        sum(one * gates[k : k + 1, :] for k, one in enumerate(picks(ids, place, chip ^ step, 0, rows)))
        for step in steps
    ]
    kept = []
    if with_x:
        plain = [picks(ids, place, e, 0, rows) for e in range(experts)]
        for k, one_ref in enumerate(ones_refs):
            one_ref[...] = jnp.concatenate([one[k] for one in plain], axis=0).astype(BF16)
        copies[3].wait()
        x_rows = dot(sum(ref[...] for ref in ones_refs), local[3][...], (1, 0))
        sends_local[-1][...] = x_rows.astype(BF16)
        kept += load([(sends_local[-1], outs[-1])], sems.at[4:])
    copies[2].wait()
    up_rows = dot(jnp.concatenate(gated, axis=0).astype(BF16), local[2][...], (1, 0)).astype(BF16)
    for b in range(len(steps)):
        sends_local[b][...] = up_rows[b * rows : (b + 1) * rows]
    kept += load(zip(sends_local[: len(steps)], outs), sems.at[5:])
    for copy in kept:
        copy.wait()


def forward_kernel(steps, chip_ref, x_ref, *refs):
    w_in_refs, (x_out, *terms), x_local, sem = refs[:2], refs[2:-2], refs[-2], refs[-1]
    half = terms[0].shape[1]
    rows = x_ref.shape[0] // len(steps)
    for b, step in enumerate(steps):
        x_local[b * rows : (b + 1) * rows, :] = x_ref[rows_of(chip_ref[0], step, rows), :]
    x_rows = x_local[...]
    kept = load([(x_local, x_out)], sem)
    for h in range(2):
        slope_ref, active_ref, hidden_ref, hidden16_ref = terms[4 * h : 4 * h + 4]
        pre = dot(x_rows, w_in_refs[h][...], (1, 0))
        gate_pre, up_pre = pre[:, :half], pre[:, half:]
        squash = jax.nn.sigmoid(gate_pre)
        active = gate_pre * squash
        hidden = active * up_pre
        slope_ref[...] = up_pre * squash * (1.0 + gate_pre * (1.0 - squash))
        active_ref[...] = active
        hidden_ref[...] = hidden
        hidden16_ref[...] = hidden.astype(BF16)
    kept[0].wait()


def backward_kernel(steps, slab, chip_ref, *refs):
    count = len(steps)
    ins, terms, (w_down, other_down, w_in, other_in) = refs[:count], refs[count : count + 6], refs[count + 6 : count + 10]
    back_out, share_out, grad_out, grad_ref, share_ref, back_ref, sems = refs[-7:]
    total = grad_ref.shape[0]
    rows = total // count
    half, width = w_down.shape
    at = 4 * half
    for b, ref in enumerate(ins):
        share_ref[b * rows : (b + 1) * rows, at:] = ref[...]
    share_ref[:, 3 * half : at] = jnp.zeros((total, half), BF16)
    gate_parts = []
    for h, (weight, grad) in enumerate(((w_down, grad_ref), (other_down, share_ref))):
        slope, active, hidden = [ref[...] for ref in terms[3 * h : 3 * h + 3]]
        pulled = dot(share_ref[:, at:], weight[...], (1, 1))
        gate_parts.append(jnp.sum(hidden * pulled, axis=1, keepdims=True))
        grad[:, :half] = (pulled * slope).astype(BF16)
        grad[:, half : 2 * half] = (pulled * active).astype(BF16)
    share_ref[:, 2 * half : 3 * half] = hidden.astype(BF16)
    kept = load([(share_ref, share_out), (grad_ref, grad_out)], sems)
    lane = lax.broadcasted_iota(jnp.int32, (total, LANES), 1)
    back_ref[:, width:] = jnp.where(
        lane == 0, gate_parts[0], jnp.where(lane == 1, gate_parts[1], 0.0)
    ).astype(BF16)
    for n, first in enumerate(range(0, width, slab)):
        cut = slice(first, first + slab)
        back = dot(grad_ref[...], w_in[cut, :], (1, 1)) + dot(share_ref[:, : 2 * half], other_in[cut, :], (1, 1))
        back_ref[:, cut] = back.astype(BF16)
        if first + slab == width:
            cut = slice(first, width + LANES)
        kept += load(
            [
                (back_ref.at[b * rows : (b + 1) * rows, cut], back_out.at[rows_of(chip_ref[0], step, rows), cut])
                for b, step in enumerate(steps)
            ],
            sems.at[2 + n * count :],
        )
    for copy in kept:
        copy.wait()


def weight_kernel(count, scale, *refs):
    out_ref, lefts, rights = refs[-1], refs[:count], refs[count:-1]
    left = jnp.concatenate([ref[...] for ref in lefts], axis=0)
    right = jnp.concatenate([ref[...] for ref in rights], axis=0)
    out_ref[...] = (dot(left, right, (0, 0)) * scale).astype(BF16)


def combine_kernel(gates_ref, rows_ref, *refs):
    ones, (out_ref, gate_ref) = refs[:-4], refs[-2:]
    width = out_ref.shape[1]
    out_ref[...] = dot(sum(one[...] for one in ones), rows_ref[:, :width], (0, 0)).astype(BF16)
    for k, one in enumerate(ones):
        terms = dot(rows_ref[:, width:], one[...], (0, 0))
        gate_ref[k : k + 1, :] = (terms[0:1, :] + terms[1:2, :]) / gates_ref[k : k + 1, :].astype(F32)


def whole():
    return pl.BlockSpec(memory_space=pltpu.VMEM)


def anywhere(free=False):
    return pl.BlockSpec(memory_space=pl.ANY if free else pltpu.HBM)


def call(kernel, out_shape, chip, args, scratch, flops, mib, near=(), free=(), far_out=()):
    nbytes = sum(a.size * a.dtype.itemsize for a in args) + sum(
        math.prod(o.shape) * jnp.dtype(o.dtype).itemsize for o in out_shape
    )
    args = [
        a if n in free else pltpu.with_memory_space_constraint(a, pltpu.VMEM if n in near else pltpu.HBM)
        for n, a in enumerate(args)
    ]
    return pl.pallas_call(
        kernel,
        out_shape=tuple(out_shape),
        in_specs=[pl.BlockSpec(memory_space=pltpu.SMEM)] * len(chip)
        + [whole() if n in near else anywhere(n in free) for n in range(len(args))],
        out_specs=tuple(anywhere() if n in far_out else whole() for n in range(len(out_shape))),
        scratch_shapes=scratch,
        compiler_params=pltpu.CompilerParams(vmem_limit_bytes=mib * MIB),
        cost_estimate=pl.CostEstimate(flops=flops, bytes_accessed=nbytes, transcendentals=0),
    )(*chip, *args)


def weight_grad(lefts, rights, scale, by_left):
    depth, columns = lefts[0][2], rights[0][2]
    grid = (depth if by_left else columns) // 512
    rows = [array.shape[0] for array, _, _ in lefts]

    def spec(operand, cut):
        array, at, size = operand
        if cut:
            return pl.BlockSpec((array.shape[0], 512), lambda i: (0, at // 512 + i))
        return pl.BlockSpec((array.shape[0], size), lambda i: (0, at // size))

    return pl.pallas_call(
        functools.partial(weight_kernel, len(lefts), scale),
        grid=(grid,),
        out_shape=pltpu.HBM((depth, columns), BF16),
        in_specs=[spec(left, by_left) for left in lefts] + [spec(right, not by_left) for right in rights],
        out_specs=pl.BlockSpec((512, columns), lambda i: (i, 0)) if by_left else pl.BlockSpec((depth, 512), lambda i: (0, i)),
        compiler_params=pltpu.CompilerParams(vmem_limit_bytes=16 * MIB),
        cost_estimate=pl.CostEstimate(
            flops=2 * sum(rows) * depth * columns,
            bytes_accessed=2 * (sum(rows) * (depth + columns) + depth * columns),
            transcendentals=0,
        ),
    )(*[array for array, _, _ in lefts + rights])


def per_device(upstream, inputs, expert_ids, gate_weights, w_in, w_down):
    devices = lax.axis_size("ep")
    experts = devices // 2
    tokens, features = upstream.shape
    choose = expert_ids.shape[1]
    routed = tokens * choose
    capacity = routed * 3 // devices
    half = w_down.shape[1]
    rows = -(-capacity // 16) * 16
    total = rows * experts
    chip = [(lax.axis_index("ep") // 2).astype(jnp.int32).reshape(1)]
    ids, gates = expert_ids.T, gate_weights.T
    factor = 1.0 / math.sqrt(2 * routed)
    steps = (*(ORDER if experts == 8 else range(1, experts)), 0)
    groups = [[2 * e + c for e in range(experts)] for c in range(2)]

    def swap(value):
        return lax.ppermute(value, "ep", [(d, d ^ 1) for d in range(devices)])

    def send(blocks):
        return {
            step: lax.ppermute(blocks[step], "ep", [(d, d ^ (2 * step)) for d in range(devices)]) if step else blocks[0]
            for step in blocks
        }

    def send_all(block):
        return lax.all_to_all(block, "ep", 0, 0, axis_index_groups=groups, tiled=True)

    def like(*values):
        return [pltpu.VMEM(value.shape, value.dtype) for value in values]

    def far(rows, width):
        return pltpu.HBM((rows, width), BF16)

    def near(rows, width, dtype=BF16):
        return pltpu.VMEM((rows, width), dtype)

    def dma(count):
        return pltpu.SemaphoreType.DMA((count,))

    w_in, w_down = w_in[0], w_down[0]
    other_in, other_down = swap(w_in), swap(w_down)

    def pack(these, with_x, held=()):
        tokens_in = [ids, gates, upstream, inputs][: 3 + with_x]
        sends = [(rows, features)] * len(these) + [(total, features)] * with_x
        return call(
            functools.partial(pack_kernel, experts, rows, these, with_x, len(held)),
            [far(*size) for size in sends] + [near(total, tokens)] * (choose * with_x),
            chip,
            [*tokens_in, *held],
            like(*tokens_in) + [near(*size) for size in sends] + [dma(5 + len(these))],
            4 * total * tokens * features,
            16,
            (),
            tuple(range(3 + with_x, 3 + with_x + len(held))),
            tuple(range(len(sends))),
        )

    early = EARLY if experts == 8 else experts // 2
    *up_sent, x_sent, one, two = pack(steps[:early], 1)
    up_sent += pack(steps[early:], 0, [other_in, other_down])
    x_rows = send_all(x_sent)
    up_blocks = send(dict(zip(steps, up_sent)))

    x_rows, *terms = call(
        functools.partial(forward_kernel, steps),
        [far(total, features)] + ([near(total, half, F32)] * 3 + [near(total, half)]) * 2,
        chip,
        [x_rows, w_in, other_in],
        [near(total, features), dma(1)],
        8 * total * half * features,
        16,
        (0, 1, 2),
        (),
        (0,),
    )
    operands = [*terms[:3], *terms[4:7], w_down, other_down, w_in, other_in]
    width, share_width = features + LANES, features + 4 * half
    back, own_share, own_grad = call(
        functools.partial(backward_kernel, steps, SLAB),
        [far(total, width), far(total, share_width), far(total, 2 * half)],
        chip,
        [*[up_blocks[step] for step in steps], *operands],
        [near(total, 2 * half), near(total, share_width), near(total, width), dma(2 + experts * features // SLAB)],
        12 * total * half * features,
        16,
        tuple(range(experts + len(operands))),
        (),
        (0, 1, 2),
    )
    returned = send_all(back)

    other_share = swap(own_share)
    x_pairs = [(x_rows, 0, features), (swap(x_rows), 0, features)]
    grad_pairs = [(own_grad, 0, 2 * half), (other_share, 0, 2 * half)]
    grad_in = weight_grad(x_pairs, grad_pairs, factor, True)
    hidden_pairs = [(terms[3], 0, half), (other_share, 2 * half, half)]
    up_pairs = [(share, 4 * half, features) for share in (own_share, other_share)]
    grad_down = weight_grad(hidden_pairs, up_pairs, factor, False)

    grad_inputs, grad_gates = call(
        combine_kernel,
        [jax.ShapeDtypeStruct((tokens, features), BF16), jax.ShapeDtypeStruct((choose, tokens), F32)],
        [],
        [gates, returned, one, two, grad_in, grad_down],
        [],
        2 * total * tokens * features,
        12,
        (0, 1, 2, 3),
    )
    return (grad_inputs, grad_gates.T, grad_in[None], grad_down[None])


def solution(mesh):
    rows = P(("grp", "ep"), None)
    return jax.shard_map(
        per_device,
        mesh=mesh,
        in_specs=(rows, rows, rows, rows, P("ep", None, None), P("ep", None, None)),
        out_specs=(rows, rows, P(("grp", "ep"), None, None), P(("grp", "ep"), None, None)),
        check_vma=False,
    )
```

```python
import functools
import math

import jax
import jax.numpy as jnp
from jax import lax
from jax.experimental import pallas as pl
from jax.experimental.pallas import tpu as pltpu
from jax.sharding import PartitionSpec as P

F32 = jnp.float32
BF16 = jnp.bfloat16
LANES = 128
MIB = 1024 * 1024
GROUPS = ((2, 1, 6, 4, 5, 7, 3, 0),)
HELD = 0
SLAB = 512
EARLY = 3


def dot(a, b, contract):
    return lax.dot_general(a, b, ((contract[:1], contract[1:]), ((), ())), preferred_element_type=F32)


def places(ids, experts):
    choose, tokens = ids.shape
    names = lax.broadcasted_iota(jnp.int32, (experts, tokens), 0)
    marks = [(names == ids[k : k + 1, :]).astype(F32) for k in range(choose)]
    earlier = lax.broadcasted_iota(jnp.int32, (tokens, tokens), 0) < lax.broadcasted_iota(
        jnp.int32, (tokens, tokens), 1
    )
    counts = dot(sum(marks).astype(BF16), earlier.astype(BF16), (1, 0))
    return [jnp.sum(counts * mark, axis=0, keepdims=True).astype(jnp.int32) for mark in marks]


def picks(ids, place, expert, first, rows):
    choose, tokens = ids.shape
    slot = lax.broadcasted_iota(jnp.int32, (rows, tokens), 0) + first
    return [
        ((ids[k : k + 1, :] == expert) & (place[k] == slot)).astype(F32) for k in range(choose)
    ]


def load(pairs, sems):
    copies = [pltpu.make_async_copy(a, b, sems.at[n]) for n, (a, b) in enumerate(pairs)]
    for copy in copies:
        copy.start()
    return copies


def targets(steps, experts, chip):
    return [chip ^ n if steps else n for n in range(experts)]


def rows_of(chip, step, rows):
    return pl.ds(pl.multiple_of((chip ^ step) * rows, 16), rows)


def pack_kernel(experts, rows, steps, with_x, held, order, chip_ref, *refs):
    hbm, refs = refs[: 3 + with_x], refs[3 + with_x + held :]
    sends, kept_ones = len(steps) + with_x, 2 * with_x
    ones_refs, refs = refs[sends : sends + kept_ones], refs[:sends] + refs[sends + kept_ones :]
    outs, local, sends_local, sems = refs[:sends], refs[sends : 2 * sends + 3 + with_x][: 3 + with_x], refs[-1 - sends : -1], refs[-1]
    copies = load(zip(hbm, local), sems)
    copies[0].wait()
    copies[1].wait()
    ids = local[0][...]
    gates = local[1][...].astype(F32)
    place = places(ids, experts)
    chip = chip_ref[0]
    gated = [
        sum(one * gates[k : k + 1, :] for k, one in enumerate(picks(ids, place, chip ^ step, 0, rows)))
        for step in steps
    ]
    kept = []
    if with_x:
        plain = [picks(ids, place, e, 0, rows) for e in range(experts)]
        ones = [picks(ids, place, chip ^ step, 0, rows) for step in order]
        for k, one_ref in enumerate(ones_refs):
            one_ref[...] = jnp.concatenate([one[k] for one in ones], axis=0).astype(BF16)
        copies[3].wait()
        x_rows = dot(jnp.concatenate([sum(one) for one in plain], axis=0).astype(BF16), local[3][...], (1, 0))
        sends_local[-1][...] = x_rows.astype(BF16)
        kept += load([(sends_local[-1], outs[-1])], sems.at[4:])
    copies[2].wait()
    up_rows = dot(jnp.concatenate(gated, axis=0).astype(BF16), local[2][...], (1, 0)).astype(BF16)
    for b in range(len(steps)):
        sends_local[b][...] = up_rows[b * rows : (b + 1) * rows]
    kept += load(zip(sends_local[: len(steps)], outs), sems.at[5:])
    for copy in kept:
        copy.wait()


def forward_kernel(steps, chip_ref, x_ref, *refs):
    w_in_refs, (x_out, *terms), x_local, sem = refs[:2], refs[2:-2], refs[-2], refs[-1]
    half = terms[0].shape[1]
    rows = x_ref.shape[0] // len(steps)
    for b, step in enumerate(steps):
        x_local[b * rows : (b + 1) * rows, :] = x_ref[rows_of(chip_ref[0], step, rows), :]
    x_rows = x_local[...]
    kept = load([(x_local, x_out)], sem)
    for h in range(2):
        slope_ref, active_ref, hidden_ref, hidden16_ref = terms[4 * h : 4 * h + 4]
        pre = dot(x_rows, w_in_refs[h][...], (1, 0))
        gate_pre, up_pre = pre[:, :half], pre[:, half:]
        squash = jax.nn.sigmoid(gate_pre)
        active = gate_pre * squash
        hidden = active * up_pre
        slope_ref[...] = up_pre * squash * (1.0 + gate_pre * (1.0 - squash))
        active_ref[...] = active
        hidden_ref[...] = hidden
        hidden16_ref[...] = hidden.astype(BF16)
    kept[0].wait()


def backward_kernel(count, first, held, *refs):
    ins, terms, (w_down, other_down, w_in, other_in) = refs[:count], refs[count : count + 6], refs[count + 6 : count + 10]
    outs, (grad_ref, share_ref, back_ref, sems) = refs[count + 10 + held : -4], refs[-4:]
    back_outs, (share_out, grad_out) = outs[:count], outs[count:]
    total = grad_ref.shape[0]
    rows = total // count
    half, width = w_down.shape
    at = 4 * half
    for b, ref in enumerate(ins):
        share_ref[b * rows : (b + 1) * rows, at:] = ref[...]
    share_ref[:, 3 * half : at] = jnp.zeros((total, half), BF16)
    gate_parts = []
    for h, (weight, grad) in enumerate(((w_down, grad_ref), (other_down, share_ref))):
        slope, active, hidden = [ref[first * rows : first * rows + total, :] for ref in terms[3 * h : 3 * h + 3]]
        pulled = dot(share_ref[:, at:], weight[...], (1, 1))
        gate_parts.append(jnp.sum(hidden * pulled, axis=1, keepdims=True))
        grad[:, :half] = (pulled * slope).astype(BF16)
        grad[:, half : 2 * half] = (pulled * active).astype(BF16)
    share_ref[:, 2 * half : 3 * half] = hidden.astype(BF16)
    kept = load([(share_ref, share_out), (grad_ref, grad_out)], sems)
    back = dot(grad_ref[...], w_in[...], (1, 1)) + dot(share_ref[:, : 2 * half], other_in[...], (1, 1))
    back_ref[:, :width] = back.astype(BF16)
    lane = lax.broadcasted_iota(jnp.int32, (total, LANES), 1)
    back_ref[:, width:] = jnp.where(
        lane == 0, gate_parts[0], jnp.where(lane == 1, gate_parts[1], 0.0)
    ).astype(BF16)
    kept += load(
        [(back_ref.at[b * rows : (b + 1) * rows, :], out) for b, out in enumerate(back_outs)], sems.at[2:]
    )
    for copy in kept:
        copy.wait()


def weight_kernel(parts, scale, *refs):
    (x_own, x_other, hidden_own), refs = refs[:3], refs[3:]
    in_out, down_out = refs[-2:]
    hidden_other, grad_own, grad_other, up_own, up_other = [refs[n * parts : (n + 1) * parts] for n in range(5)]
    for lefts, rights, out in (
        ((x_own, x_other), (*grad_own, *grad_other), in_out),
        ((hidden_own, *hidden_other), (*up_own, *up_other), down_out),
    ):
        left = jnp.concatenate([ref[...] for ref in lefts], axis=0)
        right = jnp.concatenate([ref[...] for ref in rights], axis=0)
        out[...] = (dot(left, right, (0, 0)) * scale).astype(BF16)


def combine_kernel(blocks, gates_ref, one_ref, two_ref, *refs):
    ins, (out_ref, gate_ref, rows_ref) = refs[:blocks], refs[-3:]
    width = out_ref.shape[1]
    rows = rows_ref.shape[0] // blocks
    for b, ref in enumerate(ins):
        rows_ref[b * rows : (b + 1) * rows, :] = ref[...]
    ones = (one_ref[...], two_ref[...])
    out_ref[...] = dot(sum(ones), rows_ref[:, :width], (0, 0)).astype(BF16)
    for k, one in enumerate(ones):
        terms = dot(rows_ref[:, width:], one, (0, 0))
        gate_ref[k : k + 1, :] = (terms[0:1, :] + terms[1:2, :]) / gates_ref[k : k + 1, :].astype(F32)


def whole():
    return pl.BlockSpec(memory_space=pltpu.VMEM)


def anywhere(free=False):
    return pl.BlockSpec(memory_space=pl.ANY if free else pltpu.HBM)


def call(kernel, out_shape, chip, args, scratch, flops, mib, near=(), free=(), far_out=()):
    nbytes = sum(a.size * a.dtype.itemsize for a in args) + sum(
        math.prod(o.shape) * jnp.dtype(o.dtype).itemsize for o in out_shape
    )
    args = [
        a if n in free else pltpu.with_memory_space_constraint(a, pltpu.VMEM if n in near else pltpu.HBM)
        for n, a in enumerate(args)
    ]
    return pl.pallas_call(
        kernel,
        out_shape=tuple(out_shape),
        in_specs=[pl.BlockSpec(memory_space=pltpu.SMEM)] * len(chip)
        + [whole() if n in near else anywhere(n in free) for n in range(len(args))],
        out_specs=tuple(anywhere() if n in far_out else whole() for n in range(len(out_shape))),
        scratch_shapes=scratch,
        compiler_params=pltpu.CompilerParams(vmem_limit_bytes=mib * MIB),
        cost_estimate=pl.CostEstimate(flops=flops, bytes_accessed=nbytes, transcendentals=0),
    )(*chip, *args)


def weight_grads(x_own, x_other, hidden, grads, own_shares, other_shares, scale):
    rows, features = x_own.shape
    half = hidden.shape[1]
    tile = 512
    sizes = [grad.shape[0] for grad in grads]

    def cut(at, sizes):
        return [pl.BlockSpec((n, tile), lambda i: (0, at // tile + i)) for n in sizes]

    def full(width, at, sizes):
        return [pl.BlockSpec((n, width), lambda i: (0, at // width)) for n in sizes]

    return pl.pallas_call(
        functools.partial(weight_kernel, len(sizes), scale),
        grid=(features // tile,),
        out_shape=(pltpu.HBM((features, 2 * half), BF16), pltpu.HBM((half, features), BF16)),
        in_specs=cut(0, [rows, rows])
        + full(half, 0, [rows])
        + full(half, 2 * half, sizes)
        + full(2 * half, 0, sizes + sizes)
        + cut(4 * half, sizes + sizes),
        out_specs=(
            pl.BlockSpec((tile, 2 * half), lambda i: (i, 0)),
            pl.BlockSpec((half, tile), lambda i: (0, i)),
        ),
        compiler_params=pltpu.CompilerParams(vmem_limit_bytes=24 * MIB),
        cost_estimate=pl.CostEstimate(
            flops=12 * rows * features * half,
            bytes_accessed=4 * rows * (2 * features + 3 * half) + 6 * features * half,
            transcendentals=0,
        ),
    )(x_own, x_other, hidden, *other_shares, *grads, *other_shares, *own_shares, *other_shares)


def per_device(upstream, inputs, expert_ids, gate_weights, w_in, w_down):
    devices = lax.axis_size("ep")
    experts = devices // 2
    tokens, features = upstream.shape
    choose = expert_ids.shape[1]
    routed = tokens * choose
    capacity = routed * 3 // devices
    half = w_down.shape[1]
    rows = -(-capacity // 16) * 16
    total = rows * experts
    chip = [(lax.axis_index("ep") // 2).astype(jnp.int32).reshape(1)]
    ids, gates = expert_ids.T, gate_weights.T
    factor = 1.0 / math.sqrt(2 * routed)
    parts = GROUPS if experts == 8 else ((*range(1, experts - 1), 0), (experts - 1,))
    steps = sum(parts, ())
    groups = [[2 * e + c for e in range(experts)] for c in range(2)]

    def swap(value):
        return lax.ppermute(value, "ep", [(d, d ^ 1) for d in range(devices)])

    def send(blocks):
        return {
            step: lax.ppermute(blocks[step], "ep", [(d, d ^ (2 * step)) for d in range(devices)]) if step else blocks[0]
            for step in blocks
        }

    def send_all(block):
        return lax.all_to_all(block, "ep", 0, 0, axis_index_groups=groups, tiled=True)

    def like(*values):
        return [pltpu.VMEM(value.shape, value.dtype) for value in values]

    def far(rows, width):
        return pltpu.HBM((rows, width), BF16)

    def near(rows, width, dtype=BF16):
        return pltpu.VMEM((rows, width), dtype)

    def dma(count):
        return pltpu.SemaphoreType.DMA((count,))

    w_in, w_down = w_in[0], w_down[0]
    other_in, other_down = swap(w_in), swap(w_down)

    def pack(these, with_x, held=()):
        tokens_in = [ids, gates, upstream, inputs][: 3 + with_x]
        sends = [(rows, features)] * len(these) + [(total, features)] * with_x
        return call(
            functools.partial(pack_kernel, experts, rows, these, with_x, len(held), steps),
            [far(*size) for size in sends] + [pltpu.HBM((total, tokens), BF16)] * (choose * with_x),
            chip,
            [*tokens_in, *held],
            like(*tokens_in) + [near(*size) for size in sends] + [dma(5 + len(these))],
            4 * total * tokens * features,
            16,
            (),
            tuple(range(3 + with_x, 3 + with_x + len(held))),
            tuple(range(len(sends))),
        )

    early = EARLY if experts == 8 else experts // 2
    *up_sent, x_sent, one, two = pack(steps[:early], 1)
    up_sent += pack(steps[early:], 0, [other_in, other_down])
    x_rows = send_all(x_sent)
    up_blocks = send(dict(zip(steps, up_sent)))

    x_rows, *terms = call(
        functools.partial(forward_kernel, steps),
        [far(total, features)] + ([near(total, half, F32)] * 3 + [near(total, half)]) * 2,
        chip,
        [x_rows, w_in, other_in],
        [near(total, features), dma(1)],
        8 * total * half * features,
        16,
        (0, 1, 2),
        (),
        (0,),
    )
    operands = [*terms[:3], *terms[4:7], w_down, other_down, w_in, other_in]
    width, share_width = features + LANES, features + 4 * half
    returned, shares, grads, first, held = {}, [], [], 0, []
    for part in parts:
        count, size = len(part), len(part) * rows
        *back, share, grad = call(
            functools.partial(backward_kernel, count, first, len(held)),
            [far(rows, width)] * count + [far(size, share_width), far(size, 2 * half)],
            [],
            [*[up_blocks[step] for step in part], *operands, *held],
            [near(size, 2 * half), near(size, share_width), near(size, width), dma(2 + count)],
            12 * size * half * features,
            16,
            tuple(range(count + len(operands))),
            tuple(range(count + len(operands), count + len(operands) + len(held))),
            tuple(range(count + 2)),
        )
        returned.update(send(dict(zip(part, back))))
        shares.append(share)
        grads.append(grad)
        first += count
        held = [returned[step] for step in part[:HELD]]

    other_shares = [swap(share) for share in shares]
    grad_in, grad_down = weight_grads(x_rows, swap(x_rows), terms[3], grads, shares, other_shares, factor)

    grad_inputs, grad_gates = call(
        functools.partial(combine_kernel, experts),
        [jax.ShapeDtypeStruct((tokens, features), BF16), jax.ShapeDtypeStruct((choose, tokens), F32)],
        [],
        [gates, one, two, *[returned[step] for step in steps], grad_in, grad_down],
        [near(total, width)],
        2 * total * tokens * features,
        12,
        tuple(range(3 + experts)),
    )
    return (grad_inputs, grad_gates.T, grad_in[None], grad_down[None])


def solution(mesh):
    rows = P(("grp", "ep"), None)
    return jax.shard_map(
        per_device,
        mesh=mesh,
        in_specs=(rows, rows, rows, rows, P("ep", None, None), P("ep", None, None)),
        out_specs=(rows, rows, P(("grp", "ep"), None, None), P(("grp", "ep"), None, None)),
        check_vma=False,
    )
```

```python
import functools
import math

import jax
import jax.numpy as jnp
from jax import lax
from jax.experimental import pallas as pl
from jax.experimental.pallas import tpu as pltpu
from jax.sharding import PartitionSpec as P

F32 = jnp.float32
BF16 = jnp.bfloat16
LANES = 128
MIB = 1024 * 1024
ORDER = (1, 2, 5, 7, 4, 6, 3)
BACK = (1, 2, 6, 4, 5, 7, 3)
SLAB = 512
EARLY = 3


def dot(a, b, contract):
    return lax.dot_general(a, b, ((contract[:1], contract[1:]), ((), ())), preferred_element_type=F32)


def places(ids, experts):
    choose, tokens = ids.shape
    names = lax.broadcasted_iota(jnp.int32, (experts, tokens), 0)
    marks = [(names == ids[k : k + 1, :]).astype(F32) for k in range(choose)]
    earlier = lax.broadcasted_iota(jnp.int32, (tokens, tokens), 0) < lax.broadcasted_iota(
        jnp.int32, (tokens, tokens), 1
    )
    counts = dot(sum(marks).astype(BF16), earlier.astype(BF16), (1, 0))
    return [jnp.sum(counts * mark, axis=0, keepdims=True).astype(jnp.int32) for mark in marks]


def picks(ids, place, expert, first, rows):
    choose, tokens = ids.shape
    slot = lax.broadcasted_iota(jnp.int32, (rows, tokens), 0) + first
    return [
        ((ids[k : k + 1, :] == expert) & (place[k] == slot)).astype(F32) for k in range(choose)
    ]


def load(pairs, sems):
    copies = [pltpu.make_async_copy(a, b, sems.at[n]) for n, (a, b) in enumerate(pairs)]
    for copy in copies:
        copy.start()
    return copies


def targets(steps, experts, chip):
    return [chip ^ n if steps else n for n in range(experts)]


def rows_of(chip, step, rows):
    return pl.ds(pl.multiple_of((chip ^ step) * rows, 16), rows)


def pack_kernel(experts, rows, steps, with_x, held, order, chip_ref, *refs):
    hbm, refs = refs[: 3 + with_x], refs[3 + with_x + held :]
    sends, kept_ones = len(steps) + with_x, 2 * (1 - with_x)
    ones_refs, refs = refs[sends : sends + kept_ones], refs[:sends] + refs[sends + kept_ones :]
    outs, local, sends_local, sems = refs[:sends], refs[sends : 2 * sends + 3 + with_x][: 3 + with_x], refs[-1 - sends : -1], refs[-1]
    copies = load(zip(hbm, local), sems)
    copies[0].wait()
    copies[1].wait()
    ids = local[0][...]
    gates = local[1][...].astype(F32)
    place = places(ids, experts)
    chip = chip_ref[0]
    gated = [
        sum(one * gates[k : k + 1, :] for k, one in enumerate(picks(ids, place, chip ^ step, 0, rows)))
        for step in steps
    ]
    kept = []
    if not with_x:
        ones = [picks(ids, place, chip ^ step, 0, rows) for step in order]
        for k, one_ref in enumerate(ones_refs):
            one_ref[...] = jnp.concatenate([one[k] for one in ones], axis=0).astype(BF16)
    else:
        plain = [picks(ids, place, e, 0, rows) for e in range(experts)]
        copies[3].wait()
        x_rows = dot(jnp.concatenate([sum(one) for one in plain], axis=0).astype(BF16), local[3][...], (1, 0))
        sends_local[-1][...] = x_rows.astype(BF16)
        kept += load([(sends_local[-1], outs[-1])], sems.at[4:])
    copies[2].wait()
    up_rows = dot(jnp.concatenate(gated, axis=0).astype(BF16), local[2][...], (1, 0)).astype(BF16)
    for b in range(len(steps)):
        sends_local[b][...] = up_rows[b * rows : (b + 1) * rows]
    kept += load(zip(sends_local[: len(steps)], outs), sems.at[5:])
    for copy in kept:
        copy.wait()


def forward_kernel(steps, chip_ref, x_ref, *refs):
    w_in_refs, (x_out, *terms), x_local, sem = refs[:2], refs[2:-2], refs[-2], refs[-1]
    half = terms[0].shape[1]
    rows = x_ref.shape[0] // len(steps)
    for b, step in enumerate(steps):
        x_local[b * rows : (b + 1) * rows, :] = x_ref[rows_of(chip_ref[0], step, rows), :]
    x_rows = x_local[...]
    kept = load([(x_local, x_out)], sem)
    for h in range(2):
        slope_ref, active_ref, hidden_ref, hidden16_ref = terms[4 * h : 4 * h + 4]
        pre = dot(x_rows, w_in_refs[h][...], (1, 0))
        gate_pre, up_pre = pre[:, :half], pre[:, half:]
        squash = jax.nn.sigmoid(gate_pre)
        active = gate_pre * squash
        hidden = active * up_pre
        slope_ref[...] = up_pre * squash * (1.0 + gate_pre * (1.0 - squash))
        active_ref[...] = active
        hidden_ref[...] = hidden
        hidden16_ref[...] = hidden.astype(BF16)
    kept[0].wait()


def backward_kernel(count, *refs):
    ins, terms, (w_down, other_down, w_in, other_in) = refs[:count], refs[count : count + 6], refs[count + 6 : count + 10]
    outs, (grad_ref, share_ref, back_ref, sems) = refs[count + 10 : -4], refs[-4:]
    back_outs, (share_out, grad_out) = outs[:count], outs[count:]
    total = grad_ref.shape[0]
    rows = total // count
    half, width = w_down.shape
    at = 4 * half
    for b, ref in enumerate(ins):
        share_ref[b * rows : (b + 1) * rows, at:] = ref[...]
    share_ref[:, 3 * half : at] = jnp.zeros((total, half), BF16)
    gate_parts = []
    for h, (weight, grad) in enumerate(((w_down, grad_ref), (other_down, share_ref))):
        slope, active, hidden = [ref[...] for ref in terms[3 * h : 3 * h + 3]]
        pulled = dot(share_ref[:, at:], weight[...], (1, 1))
        gate_parts.append(jnp.sum(hidden * pulled, axis=1, keepdims=True))
        grad[:, :half] = (pulled * slope).astype(BF16)
        grad[:, half : 2 * half] = (pulled * active).astype(BF16)
    share_ref[:, 2 * half : 3 * half] = hidden.astype(BF16)
    kept = load([(share_ref, share_out), (grad_ref, grad_out)], sems)
    lane = lax.broadcasted_iota(jnp.int32, (total, LANES), 1)
    back_ref[:, width:] = jnp.where(
        lane == 0, gate_parts[0], jnp.where(lane == 1, gate_parts[1], 0.0)
    ).astype(BF16)
    for n, at in enumerate(range(0, width, SLAB)):
        cut = slice(at, at + SLAB)
        back = dot(grad_ref[...], w_in[cut, :], (1, 1)) + dot(share_ref[:, : 2 * half], other_in[cut, :], (1, 1))
        back_ref[:, cut] = back.astype(BF16)
        if at + SLAB == width:
            cut = slice(at, width + LANES)
        kept += load(
            [(back_ref.at[b * rows : (b + 1) * rows, cut], out.at[:, cut]) for b, out in enumerate(back_outs)],
            sems.at[2 + n * count :],
        )
    for copy in kept:
        copy.wait()


def weight_kernel(scale, x_own, x_other, hidden_own, hidden_other, grad_own, grad_other, up_own, up_other, in_out, down_out):
    for own_left, other_left, own_right, other_right, out in (
        (x_own, x_other, grad_own, grad_other, in_out),
        (hidden_own, hidden_other, up_own, up_other, down_out),
    ):
        left = jnp.concatenate([own_left[...], other_left[...]], axis=0)
        right = jnp.concatenate([own_right[...], other_right[...]], axis=0)
        out[...] = (dot(left, right, (0, 0)) * scale).astype(BF16)


def combine_kernel(blocks, gates_ref, one_ref, two_ref, *refs):
    ins, (out_ref, gate_ref, rows_ref) = refs[:blocks], refs[-3:]
    width = out_ref.shape[1]
    rows = rows_ref.shape[0] // blocks
    for b, ref in enumerate(ins):
        rows_ref[b * rows : (b + 1) * rows, :] = ref[...]
    ones = (one_ref[...], two_ref[...])
    out_ref[...] = dot(sum(ones), rows_ref[:, :width], (0, 0)).astype(BF16)
    for k, one in enumerate(ones):
        terms = dot(rows_ref[:, width:], one, (0, 0))
        gate_ref[k : k + 1, :] = (terms[0:1, :] + terms[1:2, :]) / gates_ref[k : k + 1, :].astype(F32)


def whole():
    return pl.BlockSpec(memory_space=pltpu.VMEM)


def anywhere(free=False):
    return pl.BlockSpec(memory_space=pl.ANY if free else pltpu.HBM)


def call(kernel, out_shape, chip, args, scratch, flops, mib, near=(), free=(), far_out=()):
    nbytes = sum(a.size * a.dtype.itemsize for a in args) + sum(
        math.prod(o.shape) * jnp.dtype(o.dtype).itemsize for o in out_shape
    )
    args = [
        a if n in free else pltpu.with_memory_space_constraint(a, pltpu.VMEM if n in near else pltpu.HBM)
        for n, a in enumerate(args)
    ]
    return pl.pallas_call(
        kernel,
        out_shape=tuple(out_shape),
        in_specs=[pl.BlockSpec(memory_space=pltpu.SMEM)] * len(chip)
        + [whole() if n in near else anywhere(n in free) for n in range(len(args))],
        out_specs=tuple(anywhere() if n in far_out else whole() for n in range(len(out_shape))),
        scratch_shapes=scratch,
        compiler_params=pltpu.CompilerParams(vmem_limit_bytes=mib * MIB),
        cost_estimate=pl.CostEstimate(flops=flops, bytes_accessed=nbytes, transcendentals=0),
    )(*chip, *args)


def weight_grads(x_own, x_other, hidden, grad, own_share, other_share, scale):
    rows, features = x_own.shape
    half = hidden.shape[1]
    tile = 512

    def cut(at):
        return pl.BlockSpec((rows, tile), lambda i: (0, at // tile + i))

    def full(width, at):
        return pl.BlockSpec((rows, width), lambda i: (0, at // width))

    return pl.pallas_call(
        functools.partial(weight_kernel, scale),
        grid=(features // tile,),
        out_shape=(pltpu.HBM((features, 2 * half), BF16), pltpu.HBM((half, features), BF16)),
        in_specs=[cut(0), cut(0), full(half, 0), full(half, 2 * half), full(2 * half, 0), full(2 * half, 0)]
        + [cut(4 * half), cut(4 * half)],
        out_specs=(
            pl.BlockSpec((tile, 2 * half), lambda i: (i, 0)),
            pl.BlockSpec((half, tile), lambda i: (0, i)),
        ),
        compiler_params=pltpu.CompilerParams(vmem_limit_bytes=24 * MIB),
        cost_estimate=pl.CostEstimate(
            flops=12 * rows * features * half,
            bytes_accessed=4 * rows * (2 * features + 3 * half) + 6 * features * half,
            transcendentals=0,
        ),
    )(x_own, x_other, hidden, other_share, grad, other_share, own_share, other_share)


def per_device(upstream, inputs, expert_ids, gate_weights, w_in, w_down):
    devices = lax.axis_size("ep")
    experts = devices // 2
    tokens, features = upstream.shape
    choose = expert_ids.shape[1]
    routed = tokens * choose
    capacity = routed * 3 // devices
    half = w_down.shape[1]
    rows = -(-capacity // 16) * 16
    total = rows * experts
    chip = [(lax.axis_index("ep") // 2).astype(jnp.int32).reshape(1)]
    ids, gates = expert_ids.T, gate_weights.T
    factor = 1.0 / math.sqrt(2 * routed)
    order, order_back = (ORDER, BACK) if experts == 8 else (tuple(range(1, experts)),) * 2
    steps, steps_back = (*order, 0), (*order_back, 0)
    groups = [[2 * e + c for e in range(experts)] for c in range(2)]

    def swap(value):
        return lax.ppermute(value, "ep", [(d, d ^ 1) for d in range(devices)])

    def send(blocks):
        return {
            step: lax.ppermute(blocks[step], "ep", [(d, d ^ (2 * step)) for d in range(devices)]) if step else blocks[0]
            for step in blocks
        }

    def send_all(block):
        return lax.all_to_all(block, "ep", 0, 0, axis_index_groups=groups, tiled=True)

    def like(*values):
        return [pltpu.VMEM(value.shape, value.dtype) for value in values]

    def far(rows, width):
        return pltpu.HBM((rows, width), BF16)

    def near(rows, width, dtype=BF16):
        return pltpu.VMEM((rows, width), dtype)

    def dma(count):
        return pltpu.SemaphoreType.DMA((count,))

    w_in, w_down = w_in[0], w_down[0]
    other_in, other_down = swap(w_in), swap(w_down)

    def pack(these, with_x, held=()):
        tokens_in = [ids, gates, upstream, inputs][: 3 + with_x]
        sends = [(rows, features)] * len(these) + [(total, features)] * with_x
        return call(
            functools.partial(pack_kernel, experts, rows, these, with_x, len(held), steps_back),
            [far(*size) for size in sends] + [far(total, tokens)] * (choose * (1 - with_x)),
            chip,
            [*tokens_in, *held],
            like(*tokens_in) + [near(*size) for size in sends] + [dma(5 + len(these))],
            4 * total * tokens * features,
            16,
            (),
            tuple(range(3 + with_x, 3 + with_x + len(held))),
            tuple(range(len(sends))),
        )

    early = EARLY if experts == 8 else experts // 2
    *up_sent, x_sent = pack(steps[:early], 1)
    *rest, one, two = pack(steps[early:], 0, [other_in, other_down])
    up_sent += rest
    x_rows = send_all(x_sent)
    up_blocks = send(dict(zip(steps, up_sent)))

    x_rows, *terms = call(
        functools.partial(forward_kernel, steps),
        [far(total, features)] + ([near(total, half, F32)] * 3 + [near(total, half)]) * 2,
        chip,
        [x_rows, w_in, other_in],
        [near(total, features), dma(1)],
        8 * total * half * features,
        16,
        (0, 1, 2),
        (),
        (0,),
    )
    operands = [*terms[:3], *terms[4:7], w_down, other_down, w_in, other_in]
    width, share_width = features + LANES, features + 4 * half
    *back, share, grad = call(
        functools.partial(backward_kernel, experts),
        [far(rows, width)] * experts + [far(total, share_width), far(total, 2 * half)],
        [],
        [*[up_blocks[step] for step in steps], *operands],
        [near(total, 2 * half), near(total, share_width), near(total, width), dma(2 + experts * features // SLAB)],
        12 * total * half * features,
        16,
        tuple(range(experts + len(operands))),
        (),
        tuple(range(experts + 2)),
    )
    back = dict(zip(steps, back))
    returned = send({step: back[step] for step in steps_back})

    grad_in, grad_down = weight_grads(x_rows, swap(x_rows), terms[3], grad, share, swap(share), factor)

    grad_inputs, grad_gates = call(
        functools.partial(combine_kernel, experts),
        [jax.ShapeDtypeStruct((tokens, features), BF16), jax.ShapeDtypeStruct((choose, tokens), F32)],
        [],
        [gates, one, two, *[returned[step] for step in steps_back], grad_in, grad_down],
        [near(total, width)],
        2 * total * tokens * features,
        12,
        tuple(range(3 + experts)),
    )
    return (grad_inputs, grad_gates.T, grad_in[None], grad_down[None])


def solution(mesh):
    rows = P(("grp", "ep"), None)
    return jax.shard_map(
        per_device,
        mesh=mesh,
        in_specs=(rows, rows, rows, rows, P("ep", None, None), P("ep", None, None)),
        out_specs=(rows, rows, P(("grp", "ep"), None, None), P(("grp", "ep"), None, None)),
        check_vma=False,
    )
```

```python
import functools
import math

import jax
import jax.numpy as jnp
from jax import lax
from jax.experimental import pallas as pl
from jax.experimental.pallas import tpu as pltpu
from jax.sharding import PartitionSpec as P

F32 = jnp.float32
BF16 = jnp.bfloat16
LANES = 128
MIB = 1024 * 1024
ORDER = (1, 2, 5, 7, 4, 6, 3)
BACK = (1, 6, 2, 4, 5, 7, 3)
SLAB = 512
EARLY = 3


def dot(a, b, contract):
    return lax.dot_general(a, b, ((contract[:1], contract[1:]), ((), ())), preferred_element_type=F32)


def places(ids, experts):
    choose, tokens = ids.shape
    names = lax.broadcasted_iota(jnp.int32, (experts, tokens), 0)
    marks = [(names == ids[k : k + 1, :]).astype(F32) for k in range(choose)]
    earlier = lax.broadcasted_iota(jnp.int32, (tokens, tokens), 0) < lax.broadcasted_iota(
        jnp.int32, (tokens, tokens), 1
    )
    counts = dot(sum(marks).astype(BF16), earlier.astype(BF16), (1, 0))
    return [jnp.sum(counts * mark, axis=0, keepdims=True).astype(jnp.int32) for mark in marks]


def picks(ids, place, expert, first, rows):
    choose, tokens = ids.shape
    slot = lax.broadcasted_iota(jnp.int32, (rows, tokens), 0) + first
    return [
        ((ids[k : k + 1, :] == expert) & (place[k] == slot)).astype(F32) for k in range(choose)
    ]


def load(pairs, sems):
    copies = [pltpu.make_async_copy(a, b, sems.at[n]) for n, (a, b) in enumerate(pairs)]
    for copy in copies:
        copy.start()
    return copies


def targets(steps, experts, chip):
    return [chip ^ n if steps else n for n in range(experts)]


def rows_of(chip, step, rows):
    return pl.ds(pl.multiple_of((chip ^ step) * rows, 16), rows)


def pack_kernel(experts, rows, steps, with_x, held, order, chip_ref, *refs):
    hbm, refs = refs[: 3 + with_x], refs[3 + with_x + held :]
    sends, kept_ones = len(steps) + with_x, 2 * (1 - with_x)
    ones_refs, refs = refs[sends : sends + kept_ones], refs[:sends] + refs[sends + kept_ones :]
    outs, local, sends_local, sems = refs[:sends], refs[sends : 2 * sends + 3 + with_x][: 3 + with_x], refs[-1 - sends : -1], refs[-1]
    copies = load(zip(hbm, local), sems)
    copies[0].wait()
    copies[1].wait()
    ids = local[0][...]
    gates = local[1][...].astype(F32)
    place = places(ids, experts)
    chip = chip_ref[0]
    gated = [
        sum(one * gates[k : k + 1, :] for k, one in enumerate(picks(ids, place, chip ^ step, 0, rows)))
        for step in steps
    ]
    kept = []
    if not with_x:
        ones = [picks(ids, place, chip ^ step, 0, rows) for step in order]
        for k, one_ref in enumerate(ones_refs):
            one_ref[...] = jnp.concatenate([one[k] for one in ones], axis=0).astype(BF16)
    else:
        plain = [picks(ids, place, e, 0, rows) for e in range(experts)]
        copies[3].wait()
        x_rows = dot(jnp.concatenate([sum(one) for one in plain], axis=0).astype(BF16), local[3][...], (1, 0))
        sends_local[-1][...] = x_rows.astype(BF16)
        kept += load([(sends_local[-1], outs[-1])], sems.at[4:])
    copies[2].wait()
    up_rows = dot(jnp.concatenate(gated, axis=0).astype(BF16), local[2][...], (1, 0)).astype(BF16)
    for b in range(len(steps)):
        sends_local[b][...] = up_rows[b * rows : (b + 1) * rows]
    kept += load(zip(sends_local[: len(steps)], outs), sems.at[5:])
    for copy in kept:
        copy.wait()


def forward_kernel(steps, chip_ref, x_ref, *refs):
    w_in_refs, (x_out, *terms), x_local, sem = refs[:2], refs[2:-2], refs[-2], refs[-1]
    half = terms[0].shape[1]
    rows = x_ref.shape[0] // len(steps)
    for b, step in enumerate(steps):
        x_local[b * rows : (b + 1) * rows, :] = x_ref[rows_of(chip_ref[0], step, rows), :]
    x_rows = x_local[...]
    kept = load([(x_local, x_out)], sem)
    for h in range(2):
        slope_ref, active_ref, hidden_ref, hidden16_ref = terms[4 * h : 4 * h + 4]
        pre = dot(x_rows, w_in_refs[h][...], (1, 0))
        gate_pre, up_pre = pre[:, :half], pre[:, half:]
        squash = jax.nn.sigmoid(gate_pre)
        active = gate_pre * squash
        hidden = active * up_pre
        slope_ref[...] = up_pre * squash * (1.0 + gate_pre * (1.0 - squash))
        active_ref[...] = active
        hidden_ref[...] = hidden
        hidden16_ref[...] = hidden.astype(BF16)
    kept[0].wait()


def backward_kernel(count, *refs):
    ins, terms, (w_down, other_down, w_in, other_in) = refs[:count], refs[count : count + 6], refs[count + 6 : count + 10]
    outs, (grad_ref, share_ref, back_ref, sems) = refs[count + 10 : -4], refs[-4:]
    back_outs, (share_out, grad_out) = outs[:count], outs[count:]
    total = grad_ref.shape[0]
    rows = total // count
    half, width = w_down.shape
    at = 4 * half
    for b, ref in enumerate(ins):
        share_ref[b * rows : (b + 1) * rows, at:] = ref[...]
    share_ref[:, 3 * half : at] = jnp.zeros((total, half), BF16)
    gate_parts = []
    for h, (weight, grad) in enumerate(((w_down, grad_ref), (other_down, share_ref))):
        slope, active, hidden = [ref[...] for ref in terms[3 * h : 3 * h + 3]]
        pulled = dot(share_ref[:, at:], weight[...], (1, 1))
        gate_parts.append(jnp.sum(hidden * pulled, axis=1, keepdims=True))
        grad[:, :half] = (pulled * slope).astype(BF16)
        grad[:, half : 2 * half] = (pulled * active).astype(BF16)
    share_ref[:, 2 * half : 3 * half] = hidden.astype(BF16)
    kept = load([(share_ref, share_out), (grad_ref, grad_out)], sems)
    lane = lax.broadcasted_iota(jnp.int32, (total, LANES), 1)
    back_ref[:, width:] = jnp.where(
        lane == 0, gate_parts[0], jnp.where(lane == 1, gate_parts[1], 0.0)
    ).astype(BF16)
    for n, at in enumerate(range(0, width, SLAB)):
        cut = slice(at, at + SLAB)
        back = dot(grad_ref[...], w_in[cut, :], (1, 1)) + dot(share_ref[:, : 2 * half], other_in[cut, :], (1, 1))
        back_ref[:, cut] = back.astype(BF16)
        if at + SLAB == width:
            cut = slice(at, width + LANES)
        kept += load(
            [(back_ref.at[b * rows : (b + 1) * rows, cut], out.at[:, cut]) for b, out in enumerate(back_outs)],
            sems.at[2 + n * count :],
        )
    for copy in kept:
        copy.wait()


def weight_kernel(scale, x_own, x_other, hidden_own, hidden_other, grad_own, grad_other, up_own, up_other, in_out, down_out):
    for own_left, other_left, own_right, other_right, out in (
        (x_own, x_other, grad_own, grad_other, in_out),
        (hidden_own, hidden_other, up_own, up_other, down_out),
    ):
        left = jnp.concatenate([own_left[...], other_left[...]], axis=0)
        right = jnp.concatenate([own_right[...], other_right[...]], axis=0)
        out[...] = (dot(left, right, (0, 0)) * scale).astype(BF16)


def combine_kernel(blocks, gates_ref, one_ref, two_ref, *refs):
    ins, (out_ref, gate_ref, rows_ref) = refs[:blocks], refs[-3:]
    width = out_ref.shape[1]
    rows = rows_ref.shape[0] // blocks
    for b, ref in enumerate(ins):
        rows_ref[b * rows : (b + 1) * rows, :] = ref[...]
    ones = (one_ref[...], two_ref[...])
    out_ref[...] = dot(sum(ones), rows_ref[:, :width], (0, 0)).astype(BF16)
    for k, one in enumerate(ones):
        terms = dot(rows_ref[:, width:], one, (0, 0))
        gate_ref[k : k + 1, :] = (terms[0:1, :] + terms[1:2, :]) / gates_ref[k : k + 1, :].astype(F32)


def whole():
    return pl.BlockSpec(memory_space=pltpu.VMEM)


def anywhere(free=False):
    return pl.BlockSpec(memory_space=pl.ANY if free else pltpu.HBM)


def call(kernel, out_shape, chip, args, scratch, flops, mib, near=(), free=(), far_out=()):
    nbytes = sum(a.size * a.dtype.itemsize for a in args) + sum(
        math.prod(o.shape) * jnp.dtype(o.dtype).itemsize for o in out_shape
    )
    args = [
        a if n in free else pltpu.with_memory_space_constraint(a, pltpu.VMEM if n in near else pltpu.HBM)
        for n, a in enumerate(args)
    ]
    return pl.pallas_call(
        kernel,
        out_shape=tuple(out_shape),
        in_specs=[pl.BlockSpec(memory_space=pltpu.SMEM)] * len(chip)
        + [whole() if n in near else anywhere(n in free) for n in range(len(args))],
        out_specs=tuple(anywhere() if n in far_out else whole() for n in range(len(out_shape))),
        scratch_shapes=scratch,
        compiler_params=pltpu.CompilerParams(vmem_limit_bytes=mib * MIB),
        cost_estimate=pl.CostEstimate(flops=flops, bytes_accessed=nbytes, transcendentals=0),
    )(*chip, *args)


def weight_grads(x_own, x_other, hidden, grad, own_share, other_share, scale):
    rows, features = x_own.shape
    half = hidden.shape[1]
    tile = 512

    def cut(at):
        return pl.BlockSpec((rows, tile), lambda i: (0, at // tile + i))

    def full(width, at):
        return pl.BlockSpec((rows, width), lambda i: (0, at // width))

    return pl.pallas_call(
        functools.partial(weight_kernel, scale),
        grid=(features // tile,),
        out_shape=(pltpu.HBM((features, 2 * half), BF16), pltpu.HBM((half, features), BF16)),
        in_specs=[cut(0), cut(0), full(half, 0), full(half, 2 * half), full(2 * half, 0), full(2 * half, 0)]
        + [cut(4 * half), cut(4 * half)],
        out_specs=(
            pl.BlockSpec((tile, 2 * half), lambda i: (i, 0)),
            pl.BlockSpec((half, tile), lambda i: (0, i)),
        ),
        compiler_params=pltpu.CompilerParams(vmem_limit_bytes=24 * MIB),
        cost_estimate=pl.CostEstimate(
            flops=12 * rows * features * half,
            bytes_accessed=4 * rows * (2 * features + 3 * half) + 6 * features * half,
            transcendentals=0,
        ),
    )(x_own, x_other, hidden, other_share, grad, other_share, own_share, other_share)


def per_device(upstream, inputs, expert_ids, gate_weights, w_in, w_down):
    devices = lax.axis_size("ep")
    experts = devices // 2
    tokens, features = upstream.shape
    choose = expert_ids.shape[1]
    routed = tokens * choose
    capacity = routed * 3 // devices
    half = w_down.shape[1]
    rows = -(-capacity // 16) * 16
    total = rows * experts
    chip = [(lax.axis_index("ep") // 2).astype(jnp.int32).reshape(1)]
    ids, gates = expert_ids.T, gate_weights.T
    factor = 1.0 / math.sqrt(2 * routed)
    order, order_back = (ORDER, BACK) if experts == 8 else (tuple(range(1, experts)),) * 2
    steps, steps_back = (*order, 0), (*order_back, 0)
    groups = [[2 * e + c for e in range(experts)] for c in range(2)]

    def swap(value):
        return lax.ppermute(value, "ep", [(d, d ^ 1) for d in range(devices)])

    def send(blocks):
        return {
            step: lax.ppermute(blocks[step], "ep", [(d, d ^ (2 * step)) for d in range(devices)]) if step else blocks[0]
            for step in blocks
        }

    def send_all(block):
        return lax.all_to_all(block, "ep", 0, 0, axis_index_groups=groups, tiled=True)

    def like(*values):
        return [pltpu.VMEM(value.shape, value.dtype) for value in values]

    def far(rows, width):
        return pltpu.HBM((rows, width), BF16)

    def near(rows, width, dtype=BF16):
        return pltpu.VMEM((rows, width), dtype)

    def dma(count):
        return pltpu.SemaphoreType.DMA((count,))

    w_in, w_down = w_in[0], w_down[0]
    other_in, other_down = swap(w_in), swap(w_down)

    def pack(these, with_x, held=()):
        tokens_in = [ids, gates, upstream, inputs][: 3 + with_x]
        sends = [(rows, features)] * len(these) + [(total, features)] * with_x
        return call(
            functools.partial(pack_kernel, experts, rows, these, with_x, len(held), steps_back),
            [far(*size) for size in sends] + [far(total, tokens)] * (choose * (1 - with_x)),
            chip,
            [*tokens_in, *held],
            like(*tokens_in) + [near(*size) for size in sends] + [dma(5 + len(these))],
            4 * total * tokens * features,
            16,
            (),
            tuple(range(3 + with_x, 3 + with_x + len(held))),
            tuple(range(len(sends))),
        )

    early = EARLY if experts == 8 else experts // 2
    *up_sent, x_sent = pack(steps[:early], 1)
    *rest, one, two = pack(steps[early:], 0, [other_in, other_down])
    up_sent += rest
    x_rows = send_all(x_sent)
    up_blocks = send(dict(zip(steps, up_sent)))

    x_rows, *terms = call(
        functools.partial(forward_kernel, steps),
        [far(total, features)] + ([near(total, half, F32)] * 3 + [near(total, half)]) * 2,
        chip,
        [x_rows, w_in, other_in],
        [near(total, features), dma(1)],
        8 * total * half * features,
        16,
        (0, 1, 2),
        (),
        (0,),
    )
    operands = [*terms[:3], *terms[4:7], w_down, other_down, w_in, other_in]
    width, share_width = features + LANES, features + 4 * half
    *back, share, grad = call(
        functools.partial(backward_kernel, experts),
        [far(rows, width)] * experts + [far(total, share_width), far(total, 2 * half)],
        [],
        [*[up_blocks[step] for step in steps], *operands],
        [near(total, 2 * half), near(total, share_width), near(total, width), dma(2 + experts * features // SLAB)],
        12 * total * half * features,
        16,
        tuple(range(experts + len(operands))),
        (),
        tuple(range(experts + 2)),
    )
    back = dict(zip(steps, back))
    returned = send({step: back[step] for step in steps_back})

    grad_in, grad_down = weight_grads(x_rows, swap(x_rows), terms[3], grad, share, swap(share), factor)

    grad_inputs, grad_gates = call(
        functools.partial(combine_kernel, experts),
        [jax.ShapeDtypeStruct((tokens, features), BF16), jax.ShapeDtypeStruct((choose, tokens), F32)],
        [],
        [gates, one, two, *[returned[step] for step in steps_back], grad_in, grad_down],
        [near(total, width)],
        2 * total * tokens * features,
        12,
        tuple(range(3 + experts)),
    )
    return (grad_inputs, grad_gates.T, grad_in[None], grad_down[None])


def solution(mesh):
    rows = P(("grp", "ep"), None)
    return jax.shard_map(
        per_device,
        mesh=mesh,
        in_specs=(rows, rows, rows, rows, P("ep", None, None), P("ep", None, None)),
        out_specs=(rows, rows, P(("grp", "ep"), None, None), P(("grp", "ep"), None, None)),
        check_vma=False,
    )
```
